256 devices in a mesh: dp: 2 (over core), row: 16 (over y, x), col: 8 (over z).
Axes of the slice: x: 4, y: 4, z: 8, core: 2. Of those that a mesh axis runs over, the one named last changes fastest.
Arguments:
- activations: bfloat16 [2048, 8192], P('dp', 'col'), may hold values from -6 to 6
- grad_outputs: bfloat16 [2048, 8192], P('dp', 'row'), may hold values from -6 to 6
- act_basis: bfloat16 [8192, 8192], P('col', 'row'), may hold values from -0.0625 to 0.0625
- grad_basis: bfloat16 [8192, 8192], P('row', 'col'), may hold values from -0.0625 to 0.0625
- seq_lengths: int32 [2, 4], P('dp'), may hold values from 1 to 512, 1024 in all within a row
- old_eigen: float32 [8192, 8192], P('row', ('col', 'dp')), may hold values from 0.01 to 1
Outputs:
- new_eigen: float32 [8192, 8192], P('row', ('col', 'dp'))
The draws below stay inside these ranges and needn't reach their ends.
Inputs may be any that keep to these rules, and one draw needn't show every extreme that they name: `seq_lengths`: each row sums to 1024, and its largest entry is exactly 512.
All inputs are finite; a program needn't handle non-finite values.
Results may differ from the reference program's by a relative error of at most 0.0015.
Values may be sent and summed in bfloat16 or wider, within the bound.
A program may use at most 64 MiB of HBM per device.

```python
import math
import jax
import jax.numpy as jnp
import numpy as np
from jax import lax

D = 8192
TOK = 1024
SEQS = 4
MOST = 512
TOKENS = 2048
N_DP = 2


def block_scale(own_key, extent, split, low, high):
    def one(axis_at, blocks):
        heights = jax.random.uniform(jax.random.fold_in(jax.random.fold_in(own_key, 6), axis_at), (blocks,), jnp.float32, low / len(split), high / len(split))
        return jnp.repeat(jnp.exp(heights), extent[axis_at] // blocks).reshape((-1,) + (1,) * (len(extent) - axis_at - 1))

    gain = one(*split[0])
    for cut in split[1:]:
        gain = gain * one(*cut)
    return gain


def length_profile(amount, total, most, slope):
    portions = [(1 << 20) // math.isqrt(rank ** slope) + 1 for rank in range(2, amount + 1)]
    spare, holding = total - most - (amount - 1), [1] * (amount - 1)
    while spare > 0:
        free = [i for i in range(amount - 1) if holding[i] < most]
        whole, budget = sum([portions[i] for i in free]), spare
        for i in free:
            extra = min(most - holding[i], max(1, budget * portions[i] // whole), spare)
            holding[i] = holding[i] + extra
            spare = spare - extra
    return np.array([most] + holding)


def uneven_parts(rng, number_of, total, most, lean):
    if number_of == 2:
        one = jax.random.randint(rng, (), max(1, total - most), min(most, total - 1) + 1)
        return jnp.stack([one, total - one])
    sizes = jnp.asarray(length_profile(number_of, total, most, lean), jnp.int32)
    pairs = (number_of - 1) // 2
    giver, sink = sizes[1:1 + 2 * pairs:2], sizes[2:2 + 2 * pairs:2]
    margin = jnp.minimum(giver - 1, most - sink)
    moved = jax.random.randint(jax.random.fold_in(rng, 1), (pairs,), 0, 1 << 20) % (margin + 1)
    sizes = sizes.at[1:1 + 2 * pairs:2].set(giver - moved).at[2:2 + 2 * pairs:2].set(sink + moved)
    return sizes[jax.random.permutation(jax.random.fold_in(rng, 2), number_of)]


def scatter_about(stream_key, shape, deviation, most, shards=(), held_as=jnp.bfloat16):
    array = jax.random.normal(stream_key, shape, jnp.float32) * deviation
    if len(shards) > 0:
        array = block_scale(stream_key, shape, shards, -0.22, 0.18) * array
    return jnp.clip(array, min=-most, max=most).astype(held_as)


def setup_inputs(seed: int = 0) -> dict:
    key_list = jax.random.split(jax.random.key(seed), 7)
    return {
        "activations": scatter_about(key_list[0], (TOKENS, D), 1.0, 6.0, ((0, 2), (1, 8))),
        "grad_outputs": scatter_about(key_list[1], (TOKENS, D), 1.0, 6.0, ((0, 2), (1, 16))),
        "act_basis": scatter_about(key_list[2], (D, D), D ** -0.5, 0.0625, ((0, 8), (1, 16))),
        "grad_basis": scatter_about(key_list[3], (D, D), D ** -0.5, 0.0625, ((0, 16), (1, 8))),
        "seq_lengths": jax.vmap(lambda own: uneven_parts(own, SEQS, TOK, MOST, 2))(jax.random.split(key_list[4], N_DP)).reshape((N_DP, SEQS)).astype(jnp.int32),
        "old_eigen": jnp.clip(jnp.exp(math.log(1.0) - 4.6051702 * jax.random.uniform(key_list[5], (D, D), jnp.float32) ** block_scale(key_list[5], (D, D), ((0, 16), (1, 16)), -0.2, 0.2)), 0.01, 1.0),
    }


def reference(activations, grad_outputs, act_basis, grad_basis, seq_lengths, old_eigen):
    act_rot = jnp.dot(activations, act_basis, preferred_element_type=jnp.float32).astype(jnp.bfloat16)
    grad_rot = jnp.dot(grad_outputs, grad_basis, preferred_element_type=jnp.float32).astype(jnp.bfloat16)
    starts = (jnp.cumsum(seq_lengths, axis=1) - seq_lengths).astype(jnp.int32)
    span = TOK // 2

    def add_one(index, squares):
        replica = index // SEQS
        member = index % SEQS
        seq_start = starts[replica, member]
        seq_end = seq_start + seq_lengths[replica, member]
        window_start = jnp.minimum(seq_start, TOK - span).astype(jnp.int32)
        position = window_start + jnp.arange(span, dtype=jnp.int32)
        inside = (position >= seq_start) & (position < seq_end)
        base_row = (window_start + replica * TOK).astype(jnp.int32)
        act_block = lax.dynamic_slice_in_dim(act_rot, base_row, span, 0)
        grad_block = lax.dynamic_slice_in_dim(grad_rot, base_row, span, 0)
        act_block = jnp.where(inside[:, None], act_block, jnp.zeros((), act_block.dtype))
        coefficient = lax.dot_general(act_block, grad_block, (((0,), (0,)), ((), ())), preferred_element_type=jnp.float32)
        return squares + coefficient * coefficient

    squares = lax.fori_loop(0, N_DP * SEQS, add_one, jnp.zeros((D, D), jnp.float32))
    fresh_term = squares / (N_DP * TOK)
    return 0.9 * old_eigen + 0.1 * fresh_term
```

```python
import functools

import jax
import jax.numpy as jnp
from jax import lax
from jax.experimental import pallas as pl
from jax.experimental.pallas import tpu as pltpu
from jax.sharding import PartitionSpec as P

MESH = pl.DeviceIdType.MESH
F32 = jnp.float32
BF16 = jnp.bfloat16
FAR_FIRST = (2, 1, 3)

SCHEDULE = (
    ("a", 0), ("g", 2), ("g", 1), ("g", 3), ("a", 1), ("g", 0), ("zb", 2, 0), ("zb", 3, 1), ("xd", 0),
    ("xd", 1), ("xd", 2), ("xd", 3), ("zb", 0, 2), ("zb", 1, 3), ("zc", 2, 0), ("zc", 3, 1), ("xf", 0),
    ("xf", 1), ("zc", 0, 2), ("xf", 2), ("zc", 1, 3), ("xf", 3), ("yf", 0), ("yf", 1), ("zf", 0), ("zf", 2),
    ("yf", 2), ("zf", 1), ("zf", 3), ("m", 0), ("yf", 3), ("gy", 0), ("gy", 1), ("az", 1, 0), ("gy", 2),
    ("az", 1, 2), ("gy", 3), ("az", 1, 1), ("az", 1, 3), ("m", 1), ("m", 2), ("gx", 0), ("az", 2, 0),
    ("az", 2, 2), ("gx", 1), ("az", 2, 1), ("az", 2, 3), ("gx", 2), ("m", 3), ("m", 4), ("t", 0), ("gx", 3),
    ("t", 1), ("az", 3, 0), ("az", 3, 2), ("az", 3, 1), ("az", 3, 3), ("m", 5), ("t", 2), ("m", 6),
    ("az", 4, 0), ("az", 4, 2), ("az", 4, 1), ("az", 4, 3), ("m", 7), ("gf", 0), ("gf", 1), ("gf", 2),
    ("gf", 3), ("t", 3),
)


def kernel(
    act_hbm, gout_hbm, abasis_hbm, gbasis_hbm, lengths_hbm,
    out_ref,
    act, gout, abasis, gbasis, lengths_ref,
    pg, pa, sx1, sx2, rx1, rx2, sums, sy, ry, grad,
    sz, rz, act_t, masked, squares, sq_send, sq_recv,
    in_sem, x1_ss, x1_rs, x2_ss, x2_rs, y_ss, y_rs, gy_ss, gy_rs, gx_ss, gx_rs, gf_ss, gf_rs,
    z_ss, z_rs, az_ss, az_rs, q_ss, q_rs,
):
    d = lax.axis_index("dp")
    row = lax.axis_index("row")
    z = lax.axis_index("col")
    y, x = row // 4, row % 4

    def at_z(k):
        return (d, row, (z + k) % 8)

    def along(ab, k):
        if ab == 0:
            return (d, y * 4 + (x + k) % 4, z)
        return (d, ((y + k) % 4) * 4 + x, z)

    def across(ab, k):
        return along(1 - ab, k)

    first = (x, y)
    second = (y, x)

    loads = [
        pltpu.make_async_copy(src, dst, in_sem.at[i])
        for i, (src, dst) in enumerate(
            ((gout_hbm, gout), (gbasis_hbm, gbasis), (act_hbm, act), (abasis_hbm, abasis),
             (lengths_hbm, lengths_ref))
        )
    ]
    for i in (3, 2, 4):
        loads[i].start()

    barrier = pltpu.get_barrier_semaphore()
    partners = [at_z(1), at_z(7), at_z(2), at_z(6), (1 - d, row, z)]
    for ab in range(2):
        for k in (1, 2, 3):
            partners.append(along(ab, k))
    for p in partners:
        pl.semaphore_signal(barrier, inc=1, device_id=p, device_id_type=MESH)

    pending = []

    def loop(n, body):
        lax.fori_loop(0, n, lambda i, c: (body(i), c)[1], 0)

    def copy(src, dst, ss, rs, dev):
        return pltpu.make_async_remote_copy(
            src_ref=src, dst_ref=dst, send_sem=ss, recv_sem=rs, device_id=dev, device_id_type=MESH
        )

    def send(src, dst, ss, rs, dev):
        c = copy(src, dst, ss, rs, dev)
        c.start()
        pending.append(c)

    def arrived(dst, rs, ss, dev):
        pltpu.make_async_remote_copy(
            src_ref=dst, dst_ref=dst, send_sem=ss, recv_sem=rs, device_id=dev, device_id_type=MESH
        ).wait_recv()

    def grad_dots(rel, use):
        ca = pl.multiple_of(((x + rel) % 4) * 128, 128)
        cb = pl.multiple_of(512 + ((y + rel) % 4) * 128, 128)

        def body(t):
            lhs = gout[pl.ds(pl.multiple_of(t * 256, 256), 256)]
            rhs = jnp.concatenate([gbasis[:, pl.ds(ca, 128)], gbasis[:, pl.ds(cb, 128)]], axis=1)
            res = jnp.dot(lhs, rhs, preferred_element_type=F32)
            for ab in range(2):
                use(t, ab, res[:, ab * 128:(ab + 1) * 128].reshape(2, 128, 128))

        loop(4, body)

    def x1_copy(ab, side, t):
        return copy(sx1.at[ab, 2 * t + side], rx1.at[ab, side, t], x1_ss.at[ab, side, t],
                    x1_rs.at[ab, side, t], along(ab, 1 if side == 0 else 3))

    def grad_far():
        loads[0].wait()
        loads[1].wait()

        def use(t, ab, block):
            sx1[ab, pl.ds(2 * t, 2)] = block.astype(BF16)
            for side in range(2):
                x1_copy(ab, side, t).start()

        grad_dots(2, use)
        pending.extend((4, lambda t, ab=ab, side=side: x1_copy(ab, side, t)) for ab in range(2) for side in range(2))

    def x2_copy(ab, side, t, h):
        return copy(sx2.at[ab, side, 2 * t + h], rx2.at[ab, side, 2 * t + h], x2_ss.at[ab, side, t, h],
                    x2_rs.at[ab, side, t, h], along(ab, 1 if side == 0 else 3))

    def grad_near(side):
        def use(t, ab, block):
            pg[1 + side, ab, pl.ds(2 * t, 2)] = block
            sx2[ab, side, 2 * t + 1 - side] = block[1 - side].astype(BF16)
            x2_copy(ab, side, t, 1 - side).start()

        grad_dots(1 if side == 0 else 3, use)
        pending.extend((4, lambda t, ab=ab: x2_copy(ab, side, t, 1 - side)) for ab in range(2))

    mid, par = z // 2, z % 2

    def act_dot(first_pair):
        if first_pair:
            blocks = ((mid + 2) % 4, (mid + 1 + 2 * par) % 4)
        else:
            blocks = (mid, (mid + 3 + 2 * par) % 4)
        starts = [pl.multiple_of(b * 128, 128) for b in blocks]

        def body(t):
            rhs = jnp.concatenate([abasis[:, pl.ds(c, 128)] for c in starts], axis=1)
            lhs = act[pl.ds(pl.multiple_of(t * 256, 256), 256)]
            res = jnp.dot(lhs, rhs, preferred_element_type=F32)
            for n, b in enumerate(blocks):
                pa[b, pl.ds(2 * t, 2)] = res[:, n * 128:(n + 1) * 128].reshape(2, 128, 128)

        loop(4, body)

    def own(k, p):
        c = (z + k) % 8
        return pa[c // 2, (c % 2) * 4 + p]

    def z_dev(side):
        return at_z(1 if side == 0 else 7)

    def z_send(side, stage, p):
        k = (4, 3, 2, 1)[stage] if side == 0 else (4, 5, 6, 7)[stage]
        value = own(k, p)
        for other in {0: (), 1: (), 2: (1, 0) if p in near[side] else (1,), 3: (2,)}[stage]:
            z_arrived(side, other, p)
            value = value + rz[side, other, p].astype(F32)
        sz[side, stage, p] = value.astype(BF16)
        send(sz.at[side, stage, p], rz.at[side, stage, p], z_ss.at[side, stage, p],
             z_rs.at[side, stage, p], z_far(side) if stage == 0 else z_dev(side))

    def z_arrived(side, stage, p):
        arrived(rz.at[side, stage, p], z_rs.at[side, stage, p], z_ss.at[side, stage, p],
                z_far(side) if stage == 0 else z_dev(side))

    def z_far(side):
        return at_z(2 if side == 0 else 6)

    near = ((0, 1), (2, 3))

    def act_first():
        loads[2].wait()
        loads[3].wait()
        loads[0].start()
        loads[1].start()
        loads[4].wait()
        act_dot(True)
        pl.semaphore_wait(barrier, len(partners))
        for stage, which in ((1, 1), (0, 0), (1, 0)):
            for i in range(2):
                z_send(0, stage, near[which][i])
                z_send(1, stage, near[1 - which][i])

    def grad_last():
        def use(t, ab, block):
            pg[0, ab, pl.ds(2 * t, 2)] = block

        grad_dots(0, use)

    def x_dep(t):
        for ab in range(2):
            for side in range(2):
                b = 2 * t + side
                arrived(rx1.at[ab, side, t], x1_rs.at[ab, side, t], x1_ss.at[ab, side, t],
                        along(ab, 1 if side == 0 else 3))
                sx2[ab, side, b] = (pg[1 + side, ab, b] + rx1[ab, side, t].astype(F32)).astype(BF16)
                c = x2_copy(ab, side, t, side)
                c.start()
                pending.append(c)

    def x_fin(t):
        for ab in range(2):
            for side in range(2):
                for h in range(2):
                    arrived(rx2.at[ab, side, 2 * t + h], x2_rs.at[ab, side, t, h], x2_ss.at[ab, side, t, h],
                            along(ab, 1 if side == 0 else 3))
            s = slice(2 * t, 2 * t + 2)
            total = pg[0, ab, s] + (rx2[ab, 0, s].astype(F32) + rx2[ab, 1, s].astype(F32))
            total = total.reshape(4, 64, 128)
            sums[ab, t] = total
            sy[ab, t] = total.astype(BF16)
            for k in FAR_FIRST:
                send(sy.at[ab, t, (second[ab] + k) % 4], ry.at[ab, t, k], y_ss.at[ab, t, k], y_rs.at[ab, t, k],
                     across(ab, k))

    def z_pair(stage):
        def run(p0, p1):
            z_send(0, stage, p0)
            z_send(1, stage, p1)
        return run

    def az_send(side, step, p):
        far = step == 4
        back = 2 if far else step - 1
        c = (z - back) % 8 if side == 0 else (z + back) % 8
        send(act_t.at[c, p], act_t.at[c, p], az_ss.at[side, step - 1, p], az_rs.at[side, step - 1, p],
             z_far(side) if far else z_dev(side))

    def az_arrived(side, step, p):
        c = (z - step) % 8 if side == 0 else (z + step) % 8
        arrived(act_t.at[c, p], az_rs.at[side, step - 1, p], az_ss.at[side, step - 1, p],
                z_far(side) if step == 4 else z_dev(side))

    def z_fin(p):
        for side in range(2):
            z_arrived(side, 3, p)
        total = own(0, p) + (rz[0, 3, p].astype(F32) + rz[1, 3, p].astype(F32))
        act_t[z, p] = total.T.astype(BF16)
        for side in range(2):
            az_send(side, 1, p)

    def az(step, p):
        for side in range(2):
            if step < 4 or p in near[side]:
                az_arrived(side, step, p)
        for side in range(2):
            if step == 2 and p in near[side]:
                az_send(side, 4, p)
        for side in range(2):
            if step < 3:
                az_send(side, step + 1, p)

    def strip(ab, rel, t):
        return 4 * ab + (first[ab] + rel) % 4, 4 * t

    def y_fin(t):
        for ab in range(2):
            total = sums[ab, t, second[ab]]
            for k in (1, 3, 2):
                arrived(ry.at[ab, t, k], y_rs.at[ab, t, k], y_ss.at[ab, t, k], across(ab, k))
                total = total + ry[ab, t, k].astype(F32)
            b, r = strip(ab, 0, t)
            grad[b, r + second[ab]] = total.astype(BF16)
            part = grad.at[b, r + second[ab]]
            for k in FAR_FIRST:
                send(part, part, gy_ss.at[ab, t, k], gy_rs.at[ab, t, k], across(ab, k))

    def gy(t):
        for ab in range(2):
            b, r = strip(ab, 0, t)
            for k in (1, 3, 2):
                part = grad.at[b, r + (second[ab] + 4 - k) % 4]
                arrived(part, gy_rs.at[ab, t, k], gy_ss.at[ab, t, k], across(ab, k))
            part = grad.at[b, pl.ds(r, 4)]
            for side in range(2):
                send(part, part, gx_ss.at[ab, side, t], gx_rs.at[ab, side, t], along(ab, 1 if side == 0 else 3))

    def gx_forward(t):
        for ab in range(2):
            for side in range(2):
                b, r = strip(ab, 3 if side == 0 else 1, t)
                dev = along(ab, 1 if side == 0 else 3)
                arrived(grad.at[b, pl.ds(r, 4)], gx_rs.at[ab, side, t], gx_ss.at[ab, side, t], dev)
                part = grad.at[b, pl.ds(r + 2 * side, 2)]
                send(part, part, gf_ss.at[ab, side, t], gf_rs.at[ab, side, t], dev)

    def gf_arrived(t):
        for ab in range(2):
            for side in range(2):
                b, r = strip(ab, 2, t)
                arrived(grad.at[b, pl.ds(r + 2 * side, 2)], gf_rs.at[ab, side, t], gf_ss.at[ab, side, t],
                        along(ab, 1 if side == 0 else 3))

    toward = 1 - 2 * par
    chunks = [(z + toward * r + 8) % 8 for r in (0, 1, -1, -2, 2, 3, -3, 4)]
    places = [chunks[2 * m] // 2 for m in range(4)]
    bounds = [jnp.int32(0)]

    def mask(n):
        for s in range(5 - len(bounds)):
            bounds.append(bounds[-1] + lengths_ref[0, s])
        c = chunks[n]

        def body(p):
            start = (c % 2) * 512 + p * 128
            position = lax.broadcasted_iota(jnp.int32, (1, 128), 1) + start
            block = act_t[c, p]
            for s in range(4):
                inside = jnp.where((position >= bounds[s]) & (position < bounds[s + 1]), 1.0, 0.0).astype(BF16)
                held = block * inside
                for h in range(2):
                    masked[n // 2, h, s, :, pl.ds(pl.multiple_of(start, 128), 128)] = held[h * 64:(h + 1) * 64]

        loop(4, body)

    partner = (1 - d, row, z)

    def q_copy(m, k):
        return copy(sq_send.at[k, m], sq_recv.at[k, m], q_ss.at[k, m], q_rs.at[k, m], partner)

    def coefficients(m, k):
        blocks = (lax.rem(x + k, 4), 4 + lax.rem(y + k, 4))

        def half(h):
            lhs = masked[m, h].reshape(256, 1024)
            rhs = jnp.concatenate([grad[b].reshape(1024, 128) for b in blocks], axis=1)
            co = jnp.dot(lhs, rhs, preferred_element_type=F32)
            co = co * co
            total = (co[:64] + co[64:128]) + (co[128:192] + co[192:])
            a, b = total[:, :128], total[:, 128:]
            squares[k, m, h] = jnp.where(d == 0, a, b)
            sq_send[k, m, h] = jnp.where(d == 0, b, a).astype(BF16)

        loop(2, half)
        q_copy(m, k).start()

    def batch(n):
        if n == 0:
            loop(2, lambda i: coefficients(i, 0))
        elif n == 1:
            loop(4, lambda i: coefficients(i // 2, 1 + 2 * (i % 2)))
        elif n == 2:
            loop(3, lambda i: coefficients(2, i + i // 2))
        else:
            loop(7, lambda i: coefficients(jnp.minimum(i, 3), jnp.where(i < 3, 2, i - 3)))

    def finish(i):
        m, k = i // 4, i % 4
        q_copy(m, k).wait_recv()
        block = jnp.where(d == 0, (x + k) % 4, (y + k) % 4)
        place = jnp.where(m < 2, jnp.where(m == 0, places[0], places[1]), jnp.where(m == 2, places[2], places[3]))
        cols = pl.ds(pl.multiple_of(block * 128, 128), 128)
        for h in range(2):
            rows = pl.ds(pl.multiple_of(place * 128 + h * 64, 64), 64)
            out_ref[rows, cols] = squares[k, m, h] + sq_recv[k, m, h].astype(F32)

    def grads(rel):
        if rel == 2:
            grad_far()
        elif rel == 0:
            grad_last()
        else:
            grad_near(0 if rel == 1 else 1)

    def acts(n):
        if n == 0:
            act_first()
        else:
            act_dot(False)

    steps = {
        "a": acts, "g": grads, "zb": z_pair(2), "zc": z_pair(3), "xd": x_dep, "xf": x_fin, "zf": z_fin, "yf": y_fin,
        "az": az, "gy": gy, "gx": gx_forward, "gf": gf_arrived, "m": mask, "t": batch,
    }
    for name, *where in SCHEDULE:
        steps[name](*where)
    loop(16, finish)
    for c in pending:
        if isinstance(c, tuple):
            loop(c[0], lambda t, make=c[1]: make(t).wait_send())
        else:
            c.wait_send()
    loop(16, lambda i: q_copy(i // 4, i % 4).wait_send())


def local(activations, grad_outputs, act_basis, grad_basis, seq_lengths, old_eigen):
    vm = pltpu.VMEM
    dma = pltpu.SemaphoreType.DMA
    anywhere = pl.BlockSpec(memory_space=pltpu.HBM)
    squares = pl.pallas_call(
        kernel,
        out_shape=pltpu.VMEM((512, 512), F32),
        in_specs=[anywhere] * 5,
        out_specs=pl.BlockSpec(memory_space=pltpu.VMEM),
        scratch_shapes=[
            vm((1024, 1024), BF16), vm((1024, 512), BF16), vm((1024, 512), BF16), vm((512, 1024), BF16),
            pltpu.SMEM((1, 4), jnp.int32),
            vm((3, 2, 8, 128, 128), F32),
            vm((4, 8, 128, 128), F32),
            vm((2, 8, 128, 128), BF16),
            vm((2, 2, 8, 128, 128), BF16),
            vm((2, 2, 4, 128, 128), BF16),
            vm((2, 2, 8, 128, 128), BF16),
            vm((2, 4, 4, 64, 128), F32),
            vm((2, 4, 4, 64, 128), BF16),
            vm((2, 4, 4, 64, 128), BF16),
            vm((8, 16, 64, 128), BF16),
            vm((2, 4, 4, 128, 128), BF16),
            vm((2, 4, 4, 128, 128), BF16),
            vm((8, 4, 128, 128), BF16),
            vm((4, 2, 4, 64, 1024), BF16),
            vm((4, 4, 2, 64, 128), F32),
            vm((4, 4, 2, 64, 128), BF16),
            vm((4, 4, 2, 64, 128), BF16),
            dma((5,)),
            dma((2, 2, 4)), dma((2, 2, 4)),
            dma((2, 2, 4, 2)), dma((2, 2, 4, 2)),
            dma((2, 4, 4)), dma((2, 4, 4)),
            dma((2, 4, 4)), dma((2, 4, 4)),
            dma((2, 2, 4)), dma((2, 2, 4)),
            dma((2, 2, 4)), dma((2, 2, 4)),
            dma((2, 4, 4)), dma((2, 4, 4)),
            dma((2, 4, 4)), dma((2, 4, 4)),
            dma((4, 4)), dma((4, 4)),
        ],
        compiler_params=pltpu.CompilerParams(
            collective_id=0, has_side_effects=True, vmem_limit_bytes=48 << 20
        ),
        name="rotate_and_square",
    )(*(pltpu.with_memory_space_constraint(a, pltpu.HBM)
        for a in (activations, grad_outputs, act_basis, grad_basis, seq_lengths)))
    return 0.9 * old_eigen + (0.1 / 2048.0) * squares


def solution(mesh):
    return jax.shard_map(
        local,
        mesh=mesh,
        in_specs=(
            P("dp", "col"),
            P("dp", "row"),
            P("col", "row"),
            P("row", "col"),
            P("dp", None),
            P("row", ("col", "dp")),
        ),
        out_specs=P("row", ("col", "dp")),
        check_vma=False,
    )
```

```python
import functools

import jax
import jax.numpy as jnp
from jax import lax
from jax.experimental import pallas as pl
from jax.experimental.pallas import tpu as pltpu
from jax.sharding import PartitionSpec as P

MESH = pl.DeviceIdType.MESH
F32 = jnp.float32
BF16 = jnp.bfloat16
FAR_FIRST = (2, 1, 3)

SCHEDULE = (
    ("a", 0), ("g", 2), ("g", 1), ("g", 3), ("a", 1), ("g", 0), ("zb", 2, 0), ("zb", 3, 1), ("xd", 0),
    ("xd", 1), ("xd", 2), ("zb", 0, 2), ("xd", 3), ("zb", 1, 3), ("zc", 2, 0), ("zc", 3, 1), ("zc", 0, 2),
    ("xf", 0), ("zc", 1, 3), ("xf", 1), ("xf", 2), ("xf", 3), ("zf", 0), ("zf", 2), ("zf", 1), ("yf", 0),
    ("zf", 3), ("d", "zb", 1, 3), ("m", 0), ("yf", 1), ("yf", 2), ("yf", 3), ("az", 1, 0), ("az", 1, 2), ("gy", 0), ("az", 1, 1),
    ("gy", 1), ("az", 1, 3), ("m", 1), ("m", 2), ("d", "xf", 3), ("gy", 2), ("az", 2, 0), ("gy", 3), ("az", 2, 2),
    ("az", 2, 1), ("gx", 0), ("az", 2, 3), ("gx", 1), ("gx", 2), ("gx", 3), ("m", 3), ("d", "az", 1, 3), ("t", 0), ("m", 4),
    ("az", 3, 0), ("az", 3, 2), ("az", 3, 1), ("az", 3, 3), ("m", 5), ("t", 1), ("m", 6), ("az", 4, 0),
    ("az", 4, 2), ("az", 4, 1), ("az", 4, 3), ("m", 7), ("t", 2), ("d", "gx", 2), ("gf", 0), ("gf", 1), ("gf", 2), ("gf", 3),
    ("t", 3),
)


def kernel(
    act_hbm, gout_hbm, abasis_hbm, gbasis_hbm, lengths_hbm,
    out_ref,
    act, gout, abasis, gbasis, lengths_ref,
    pg, pa, sx1, sx2, rx1, rx2, sums, sy, ry, grad,
    sz, rz, act_t, masked, squares, sq_send, sq_recv,
    in_sem, x1_ss, x1_rs, x2_ss, x2_rs, y_ss, y_rs, gy_ss, gy_rs, gx_ss, gx_rs, gf_ss, gf_rs,
    z_ss, z_rs, az_ss, az_rs, q_ss, q_rs,
):
    d = lax.axis_index("dp")
    row = lax.axis_index("row")
    z = lax.axis_index("col")
    y, x = row // 4, row % 4

    def at_z(k):
        return (d, row, (z + k) % 8)

    def along(ab, k):
        if ab == 0:
            return (d, y * 4 + (x + k) % 4, z)
        return (d, ((y + k) % 4) * 4 + x, z)

    def across(ab, k):
        return along(1 - ab, k)

    first = (x, y)
    second = (y, x)

    mid, par = z // 2, z % 2
    act_blocks = ((mid + 2) % 4, (mid + 1 + 2 * par) % 4, mid, (mid + 3 + 2 * par) % 4)

    def columns(ref, b):
        return ref.at[:, pl.ds(pl.multiple_of(b * 128, 128), 128)]

    def quarter(ref, t):
        return ref.at[t * 256:(t + 1) * 256]

    pairs = [(columns(abasis_hbm, b), columns(abasis, b)) for b in act_blocks[:2]]
    pairs += [(quarter(act_hbm, t), quarter(act, t)) for t in range(4)]
    pairs += [(lengths_hbm, lengths_ref), (gbasis_hbm, gbasis)]
    pairs += [(quarter(gout_hbm, t), quarter(gout, t)) for t in range(4)]
    pairs += [(columns(abasis_hbm, b), columns(abasis, b)) for b in act_blocks[2:]]
    loads = [pltpu.make_async_copy(src, dst, in_sem.at[i]) for i, (src, dst) in enumerate(pairs)]
    for c in loads:
        c.start()

    barrier = pltpu.get_barrier_semaphore()
    partners = [at_z(1), at_z(7), at_z(2), at_z(6), (1 - d, row, z)]
    for ab in range(2):
        for k in (1, 2, 3):
            partners.append(along(ab, k))
    for p in partners:
        pl.semaphore_signal(barrier, inc=1, device_id=p, device_id_type=MESH)

    pending = []

    def loop(n, body):
        lax.fori_loop(0, n, lambda i, c: (body(i), c)[1], 0)

    def copy(src, dst, ss, rs, dev):
        return pltpu.make_async_remote_copy(
            src_ref=src, dst_ref=dst, send_sem=ss, recv_sem=rs, device_id=dev, device_id_type=MESH
        )

    def send(src, dst, ss, rs, dev):
        c = copy(src, dst, ss, rs, dev)
        c.start()
        pending.append(c)

    def arrived(dst, rs, ss, dev):
        pltpu.make_async_remote_copy(
            src_ref=dst, dst_ref=dst, send_sem=ss, recv_sem=rs, device_id=dev, device_id_type=MESH
        ).wait_recv()

    def grad_dot(rel, rows):
        ca = pl.multiple_of(((x + rel) % 4) * 128, 128)
        cb = pl.multiple_of(512 + ((y + rel) % 4) * 128, 128)
        rhs = jnp.concatenate([gbasis[:, pl.ds(ca, 128)], gbasis[:, pl.ds(cb, 128)]], axis=1)
        res = jnp.dot(gout[rows], rhs, preferred_element_type=F32)
        return [res[:, ab * 128:(ab + 1) * 128].reshape(-1, 128, 128) for ab in range(2)]

    def x1_copy(ab, side, t):
        return copy(sx1.at[ab, 2 * t + side], rx1.at[ab, side, t], x1_ss.at[ab, side, t],
                    x1_rs.at[ab, side, t], along(ab, 1 if side == 0 else 3))

    def grad_far():
        loads[6].wait()
        loads[7].wait()
        for t in range(4):
            loads[8 + t].wait()
            for ab, block in enumerate(grad_dot(2, slice(t * 256, (t + 1) * 256))):
                sx1[ab, 2 * t:2 * t + 2] = block.astype(BF16)
            for ab in range(2):
                for side in range(2):
                    c = x1_copy(ab, side, t)
                    c.start()
                    pending.append(c)

    def x2_copy(ab, side, t, h):
        return copy(sx2.at[ab, side, 2 * t + h], rx2.at[ab, side, 2 * t + h], x2_ss.at[ab, side, t, h],
                    x2_rs.at[ab, side, t, h], along(ab, 1 if side == 0 else 3))

    def grad_near(side):
        for ab, block in enumerate(grad_dot(1 if side == 0 else 3, slice(0, 1024))):
            pg[1 + side, ab] = block
            sx2[ab, side] = block.astype(BF16)
        for t in range(4):
            for ab in range(2):
                c = x2_copy(ab, side, t, 1 - side)
                c.start()
                pending.append(c)

    def act_dot(first_pair):
        for i in range(6) if first_pair else (12, 13):
            loads[i].wait()
        blocks = act_blocks[:2] if first_pair else act_blocks[2:]
        rhs = jnp.concatenate([abasis[:, pl.ds(pl.multiple_of(b * 128, 128), 128)] for b in blocks], axis=1)
        res = jnp.dot(act[...], rhs, preferred_element_type=F32)
        for n, b in enumerate(blocks):
            pa[b] = res[:, n * 128:(n + 1) * 128].reshape(8, 128, 128)

    def own(k, p):
        c = (z + k) % 8
        return pa[c // 2, (c % 2) * 4 + p]

    def z_dev(side):
        return at_z(1 if side == 0 else 7)

    def z_send(side, stage, p):
        k = (4, 3, 2, 1)[stage] if side == 0 else (4, 5, 6, 7)[stage]
        value = own(k, p)
        for other in {0: (), 1: (), 2: (1, 0) if p in near[side] else (1,), 3: (2,)}[stage]:
            z_arrived(side, other, p)
            value = value + rz[side, other, p].astype(F32)
        sz[side, stage, p] = value.astype(BF16)
        send(sz.at[side, stage, p], rz.at[side, stage, p], z_ss.at[side, stage, p],
             z_rs.at[side, stage, p], z_far(side) if stage == 0 else z_dev(side))

    def z_arrived(side, stage, p):
        arrived(rz.at[side, stage, p], z_rs.at[side, stage, p], z_ss.at[side, stage, p],
                z_far(side) if stage == 0 else z_dev(side))

    def z_far(side):
        return at_z(2 if side == 0 else 6)

    near = ((0, 1), (2, 3))

    def act_first():
        act_dot(True)
        pl.semaphore_wait(barrier, len(partners))
        for stage, which in ((1, 1), (0, 0), (1, 0)):
            for i in range(2):
                z_send(0, stage, near[which][i])
                z_send(1, stage, near[1 - which][i])

    def grad_last():
        for ab, block in enumerate(grad_dot(0, slice(0, 1024))):
            pg[0, ab] = block

    def x_dep(t):
        for ab in range(2):
            for side in range(2):
                b = 2 * t + side
                arrived(rx1.at[ab, side, t], x1_rs.at[ab, side, t], x1_ss.at[ab, side, t],
                        along(ab, 1 if side == 0 else 3))
                sx2[ab, side, b] = (pg[1 + side, ab, b] + rx1[ab, side, t].astype(F32)).astype(BF16)
                c = x2_copy(ab, side, t, side)
                c.start()
                pending.append(c)

    def x_fin(t):
        for ab in range(2):
            for side in range(2):
                for h in range(2):
                    arrived(rx2.at[ab, side, 2 * t + h], x2_rs.at[ab, side, t, h], x2_ss.at[ab, side, t, h],
                            along(ab, 1 if side == 0 else 3))
            s = slice(2 * t, 2 * t + 2)
            total = pg[0, ab, s] + (rx2[ab, 0, s].astype(F32) + rx2[ab, 1, s].astype(F32))
            total = total.reshape(4, 64, 128)
            sums[ab, t] = total
            sy[ab, t] = total.astype(BF16)
            for k in FAR_FIRST:
                send(sy.at[ab, t, (second[ab] + k) % 4], ry.at[ab, t, k], y_ss.at[ab, t, k], y_rs.at[ab, t, k],
                     across(ab, k))

    def z_pair(stage):
        def run(p0, p1):
            z_send(0, stage, p0)
            z_send(1, stage, p1)
        return run

    def az_send(side, step, p):
        far = step == 4
        back = 2 if far else step - 1
        c = (z - back) % 8 if side == 0 else (z + back) % 8
        send(act_t.at[c, p], act_t.at[c, p], az_ss.at[side, step - 1, p], az_rs.at[side, step - 1, p],
             z_far(side) if far else z_dev(side))

    def az_arrived(side, step, p):
        c = (z - step) % 8 if side == 0 else (z + step) % 8
        arrived(act_t.at[c, p], az_rs.at[side, step - 1, p], az_ss.at[side, step - 1, p],
                z_far(side) if step == 4 else z_dev(side))

    def z_fin(p):
        for side in range(2):
            z_arrived(side, 3, p)
        total = own(0, p) + (rz[0, 3, p].astype(F32) + rz[1, 3, p].astype(F32))
        act_t[z, p] = total.T.astype(BF16)
        for side in range(2):
            az_send(side, 1, p)

    def az(step, p):
        for side in range(2):
            if step < 4 or p in near[side]:
                az_arrived(side, step, p)
        for side in range(2):
            if step == 2 and p in near[side]:
                az_send(side, 4, p)
        for side in range(2):
            if step < 3:
                az_send(side, step + 1, p)

    def strip(ab, rel, t):
        return 4 * ab + (first[ab] + rel) % 4, 4 * t

    def y_fin(t):
        for ab in range(2):
            total = sums[ab, t, second[ab]]
            for k in (1, 3, 2):
                arrived(ry.at[ab, t, k], y_rs.at[ab, t, k], y_ss.at[ab, t, k], across(ab, k))
                total = total + ry[ab, t, k].astype(F32)
            b, r = strip(ab, 0, t)
            grad[b, r + second[ab]] = total.astype(BF16)
            part = grad.at[b, r + second[ab]]
            for k in FAR_FIRST:
                send(part, part, gy_ss.at[ab, t, k], gy_rs.at[ab, t, k], across(ab, k))

    def gy(t):
        for ab in range(2):
            b, r = strip(ab, 0, t)
            for k in (1, 3, 2):
                part = grad.at[b, r + (second[ab] + 4 - k) % 4]
                arrived(part, gy_rs.at[ab, t, k], gy_ss.at[ab, t, k], across(ab, k))
            part = grad.at[b, pl.ds(r, 4)]
            for side in range(2):
                send(part, part, gx_ss.at[ab, side, t], gx_rs.at[ab, side, t], along(ab, 1 if side == 0 else 3))

    def gx_forward(t):
        for ab in range(2):
            for side in range(2):
                b, r = strip(ab, 3 if side == 0 else 1, t)
                dev = along(ab, 1 if side == 0 else 3)
                arrived(grad.at[b, pl.ds(r, 4)], gx_rs.at[ab, side, t], gx_ss.at[ab, side, t], dev)
                part = grad.at[b, pl.ds(r + 2 * side, 2)]
                send(part, part, gf_ss.at[ab, side, t], gf_rs.at[ab, side, t], dev)

    def gf_arrived(t):
        for ab in range(2):
            for side in range(2):
                b, r = strip(ab, 2, t)
                arrived(grad.at[b, pl.ds(r + 2 * side, 2)], gf_rs.at[ab, side, t], gf_ss.at[ab, side, t],
                        along(ab, 1 if side == 0 else 3))

    toward = 1 - 2 * par
    chunks = [(z + toward * r + 8) % 8 for r in (0, 1, -1, -2, 2, 3, -3, 4)]
    places = [chunks[2 * m] // 2 for m in range(4)]
    bounds = [jnp.int32(0)]

    def mask(n):
        for s in range(5 - len(bounds)):
            bounds.append(bounds[-1] + lengths_ref[0, s])
        c = chunks[n]

        def body(p):
            start = (c % 2) * 512 + p * 128
            position = lax.broadcasted_iota(jnp.int32, (1, 128), 1) + start
            block = act_t[c, p]
            for s in range(4):
                inside = jnp.where((position >= bounds[s]) & (position < bounds[s + 1]), 1.0, 0.0).astype(BF16)
                masked[n // 2, s, :, pl.ds(pl.multiple_of(start, 128), 128)] = block * inside

        loop(4, body)

    partner = (1 - d, row, z)

    def q_copy(m, k):
        return copy(sq_send.at[k, m], sq_recv.at[k, m], q_ss.at[k, m], q_rs.at[k, m], partner)

    def coefficients(m, k):
        blocks = ((x + k) % 4, 4 + (y + k) % 4)
        lhs = masked[m].reshape(512, 1024)
        rhs = jnp.concatenate([grad[b].reshape(1024, 128) for b in blocks], axis=1)
        co = jnp.dot(lhs, rhs, preferred_element_type=F32)
        co = co * co
        total = (co[:128] + co[128:256]) + (co[256:384] + co[384:])
        a, b = total[:, :128], total[:, 128:]
        squares[k, m] = jnp.where(d == 0, a, b)
        sq_send[k, m] = jnp.where(d == 0, b, a).astype(BF16)

    tiles = (
        ((0, 0), (0, 1), (0, 3), (1, 0), (1, 1), (1, 3)),
        ((2, 0), (2, 1), (2, 3)),
        ((3, 0), (3, 1), (3, 3)),
        ((0, 2), (1, 2), (2, 2), (3, 2)),
    )

    def batch(n):
        if n == 0:
            loop(6, lambda i: coefficients(i // 3, i % 3 + i % 3 // 2))
        elif n == 3:
            loop(4, lambda i: coefficients(i, 2))
        else:
            loop(3, lambda i: coefficients(n + 1, i + i // 2))
        for m, k in tiles[n]:
            c = q_copy(m, k)
            c.start()
            pending.append(c)

    def finish(n):
        for m, k in tiles[n]:
            q_copy(m, k).wait_recv()
        for m, k in tiles[n]:
            block = jnp.where(d == 0, (x + k) % 4, (y + k) % 4)
            cols = pl.ds(pl.multiple_of(block * 128, 128), 128)
            rows = pl.ds(pl.multiple_of(places[m] * 128, 128), 128)
            out_ref[rows, cols] = squares[k, m] + sq_recv[k, m].astype(F32)

    def grads(rel):
        if rel == 2:
            grad_far()
        elif rel == 0:
            grad_last()
        else:
            grad_near(0 if rel == 1 else 1)

    def acts(n):
        if n == 0:
            act_first()
        else:
            act_dot(False)

    steps = {
        "a": acts, "g": grads, "zb": z_pair(2), "zc": z_pair(3), "xd": x_dep, "xf": x_fin, "zf": z_fin, "yf": y_fin,
        "az": az, "gy": gy, "gx": gx_forward, "gf": gf_arrived, "m": mask, "t": batch,
    }
    issued, done = {}, [0]

    def drain(count):
        while done[0] < count:
            pending[done[0]].wait_send()
            done[0] += 1

    for name, *where in SCHEDULE:
        if name == "d":
            drain(issued[tuple(where)])
        else:
            steps[name](*where)
            issued[(name, *where)] = len(pending)
    for n in range(4):
        finish(n)
    drain(len(pending))


def local(activations, grad_outputs, act_basis, grad_basis, seq_lengths, old_eigen):
    vm = pltpu.VMEM
    dma = pltpu.SemaphoreType.DMA
    anywhere = pl.BlockSpec(memory_space=pltpu.HBM)
    squares = pl.pallas_call(
        kernel,
        out_shape=pltpu.VMEM((512, 512), F32),
        in_specs=[anywhere] * 5,
        out_specs=pl.BlockSpec(memory_space=pltpu.VMEM),
        scratch_shapes=[
            vm((1024, 1024), BF16), vm((1024, 512), BF16), vm((1024, 512), BF16), vm((512, 1024), BF16),
            pltpu.SMEM((1, 4), jnp.int32),
            vm((3, 2, 8, 128, 128), F32),
            vm((4, 8, 128, 128), F32),
            vm((2, 8, 128, 128), BF16),
            vm((2, 2, 8, 128, 128), BF16),
            vm((2, 2, 4, 128, 128), BF16),
            vm((2, 2, 8, 128, 128), BF16),
            vm((2, 4, 4, 64, 128), F32),
            vm((2, 4, 4, 64, 128), BF16),
            vm((2, 4, 4, 64, 128), BF16),
            vm((8, 16, 64, 128), BF16),
            vm((2, 4, 4, 128, 128), BF16),
            vm((2, 4, 4, 128, 128), BF16),
            vm((8, 4, 128, 128), BF16),
            vm((4, 4, 128, 1024), BF16),
            vm((4, 4, 128, 128), F32),
            vm((4, 4, 128, 128), BF16),
            vm((4, 4, 128, 128), BF16),
            dma((14,)),
            dma((2, 2, 4)), dma((2, 2, 4)),
            dma((2, 2, 4, 2)), dma((2, 2, 4, 2)),
            dma((2, 4, 4)), dma((2, 4, 4)),
            dma((2, 4, 4)), dma((2, 4, 4)),
            dma((2, 2, 4)), dma((2, 2, 4)),
            dma((2, 2, 4)), dma((2, 2, 4)),
            dma((2, 4, 4)), dma((2, 4, 4)),
            dma((2, 4, 4)), dma((2, 4, 4)),
            dma((4, 4)), dma((4, 4)),
        ],
        compiler_params=pltpu.CompilerParams(
            collective_id=0, has_side_effects=True, vmem_limit_bytes=48 << 20
        ),
        name="rotate_and_square",
    )(*(pltpu.with_memory_space_constraint(a, pltpu.HBM)
        for a in (activations, grad_outputs, act_basis, grad_basis, seq_lengths)))
    return 0.9 * old_eigen + (0.1 / 2048.0) * squares


def solution(mesh):
    return jax.shard_map(
        local,
        mesh=mesh,
        in_specs=(
            P("dp", "col"),
            P("dp", "row"),
            P("col", "row"),
            P("row", "col"),
            P("dp", None),
            P("row", ("col", "dp")),
        ),
        out_specs=P("row", ("col", "dp")),
        check_vma=False,
    )
```
